128 devices in a mesh: gx: 32 (over y, x, core), gy: 4 (over z).
Axes of the slice: x: 4, y: 4, z: 4, core: 2. Of those that a mesh axis runs over, the one named last changes fastest.
Arguments:
- velocity: bfloat16 [3, 4, 4096, 2048], P(None, None, 'gx', 'gy'), may hold values from -24 to 24
- block_ids: int32 [32, 4, 128, 4], P('gx', 'gy'), may hold values from 0 to 1023
- counts: int32 [32, 4, 128], P('gx', 'gy'), may hold values from 0 to 4, as said below
- positions: float32 [3, 32, 4, 128, 128], P(None, 'gx', 'gy'), may hold values from 0 to 1
Outputs:
- filtered: bfloat16 [2, 3, 4, 4096, 2048], P(None, None, None, 'gx', 'gy')
- sampled: float32 [2, 3, 32, 4, 128, 128], P(None, None, 'gx', 'gy')
The draws below stay inside these ranges and needn't reach their ends.
Inputs may be any that keep to these rules, and one draw needn't show every extreme that they name: `block_ids`: a listed block number of the sending device. `counts`: used slots from a device to an owner; some owners get 4 from every device.
All inputs are finite; a program needn't handle non-finite values.
Results may differ from the reference program's by a relative error of at most 0.006.
Values may be sent and summed in bfloat16 or wider, within the bound.
A program may use at most 128 MiB of HBM per device.

```python
import jax
import jax.numpy as jnp
from jax import lax

CX = 128
CY = 512
CZ = 4
REACH = 8
BLOCK = 8
CAP = 4
TPB = 32
CAPT = 128
NBLK = 1024
NX = 4096
NY = 2048
N_GX = 32
N_GY = 4


def draw_counts(key, part):
    shuffled = jax.random.permutation(jax.random.fold_in(key, 11), N_GX * N_GY)
    heavy_owner = shuffled < max(1, N_GX * N_GY // 8)
    drawn = jax.random.randint(jax.random.fold_in(key, 12), (N_GX, N_GY, N_GX * N_GY), 0, CAP + 1)
    return jnp.where(heavy_owner[None, None, :], CAP, drawn).astype(jnp.int32)


def with_ends(array, key, low, top_value):
    dims = array.shape
    place = [jax.random.randint(jax.random.fold_in(key, axis), (), 0, dims[axis]) for axis in range(len(dims))]
    array = array.at[tuple(place)].set(low)
    longest = dims.index(max(dims))
    place[longest] = (place[longest] + 1) % dims[longest]
    return array.at[tuple(place)].set(top_value)


def steps_of(key, shape, cuts, least, largest):
    factor_of, own = 1.0, jax.random.fold_in(key, 6)
    for dim, parts in cuts:
        steps = jnp.exp(jax.random.uniform(jax.random.fold_in(own, dim), (parts,), jnp.float32, least / len(cuts), largest / len(cuts)))
        factor_of = factor_of * jnp.repeat(steps, shape[dim] // parts).reshape([-1 if axis == dim else 1 for axis in range(len(shape))])
    return factor_of


def bell_draw(stream_key, shape, scale, bound, cuts=(), held_as=jnp.bfloat16):
    level = steps_of(stream_key, shape, cuts, -0.22, 0.18) if cuts else 1.0
    entries = jax.random.normal(stream_key, shape, jnp.float32) * scale * level
    return jnp.minimum(jnp.maximum(entries, -bound), bound).astype(held_as)


def setup_inputs(seed: int = 0) -> dict:
    splits = jax.random.split(jax.random.key(seed), 5)
    velocity = bell_draw(splits[0], (3, CZ, NX, NY), 4.0, 24.0, ((2, 32), (3, 4)))
    block_ids = with_ends(jax.random.randint(splits[1], (N_GX, N_GY, N_GX * N_GY, CAP), 0, NBLK), jax.random.fold_in(splits[1], 1), 0, NBLK - 1).astype(jnp.int32)
    counts = draw_counts(jax.random.fold_in(splits[4], 71), 0)
    positions = jnp.clip(1.0 * jax.random.uniform(splits[3], (3, N_GX, N_GY, N_GX * N_GY, CAPT), jnp.float32) ** steps_of(splits[3], (3, N_GX, N_GY, N_GX * N_GY, CAPT), ((1, 32), (2, 4)), -0.2, 0.2), 0.0, 1.0)
    return {"velocity": velocity, "block_ids": block_ids, "counts": counts, "positions": positions}


SIGMAS = (1.5, 3.0)


def make_taps():
    offsets = jnp.arange(2 * REACH + 1, dtype=jnp.float32) - float(REACH)
    stacked = []
    for deviation in SIGMAS:
        profile = jnp.exp(-offsets * offsets / (2.0 * deviation * deviation))
        stacked.append(profile / jnp.sum(profile))
    return jnp.stack(stacked).astype(jnp.bfloat16)


def smooth_axis(field_plane, tap_row, direction):
    running = jnp.zeros(field_plane.shape, jnp.float32)
    for offset in range(2 * REACH + 1):
        moved = jnp.roll(field_plane, REACH - offset, axis=direction)
        running = running + tap_row[offset].astype(jnp.float32) * moved.astype(jnp.float32)
    return running.astype(jnp.bfloat16)


def interpolate(blocks, spots):
    cell_axis = jnp.arange(BLOCK, dtype=jnp.float32)
    plane_axis = jnp.arange(CZ, dtype=jnp.float32)
    weight_x = jnp.maximum(0.0, 1.0 - jnp.abs(spots[0][..., None] * (BLOCK - 1) - cell_axis))
    weight_y = jnp.maximum(0.0, 1.0 - jnp.abs(spots[1][..., None] * (BLOCK - 1) - cell_axis))
    weight_z = jnp.maximum(0.0, 1.0 - jnp.abs(spots[2][..., None] * (CZ - 1) - plane_axis))
    result = jnp.einsum("sjwczab,sjtz,sjta,sjtb->wcsjt", blocks.astype(jnp.float32), weight_z, weight_x, weight_y, precision=lax.Precision.HIGHEST)
    return result.reshape(2, 3, blocks.shape[0], -1)


def reference(velocity, block_ids, counts, positions):
    tap_table = make_taps()
    devices_all = N_GX * N_GY

    def smooth_plane(field_plane):
        both = []
        for width in range(2):
            along_y = smooth_axis(field_plane, tap_table[width], 1)
            both.append(smooth_axis(along_y, tap_table[width], 0))
        return jnp.stack(both)

    planes = velocity.reshape(3 * CZ, NX, NY)
    smoothed = lax.map(smooth_plane, planes)
    filtered = smoothed.reshape(3, CZ, 2, NX, NY).transpose(2, 0, 1, 3, 4)
    tiled = filtered.reshape(2, 3, CZ, N_GX, CX // BLOCK, BLOCK, N_GY, CY // BLOCK, BLOCK)
    blocks_all = tiled.transpose(3, 6, 4, 7, 0, 1, 2, 5, 8).reshape(devices_all, NBLK, 2, 3, CZ, BLOCK, BLOCK)
    id_table = block_ids.reshape(devices_all, devices_all, CAP)
    used_table = counts.reshape(devices_all, devices_all)
    spot_table = positions.reshape(3, devices_all, devices_all, CAP, TPB).transpose(1, 0, 2, 3, 4)
    sources = jnp.arange(devices_all, dtype=jnp.int32)
    slot_axis = jnp.arange(CAP, dtype=jnp.int32)

    def one_owner(inputs):
        owner_spots, owner = inputs
        listed = id_table[:, owner, :]
        live = (slot_axis[None, :] < used_table[:, owner][:, None]).astype(jnp.bfloat16)
        chosen = blocks_all[sources[:, None], listed]
        chosen = chosen * live[:, :, None, None, None, None, None]
        return interpolate(chosen, owner_spots)

    per_owner = lax.map(one_owner, (spot_table, sources))
    sampled = per_owner.transpose(1, 2, 0, 3, 4).reshape(2, 3, N_GX, N_GY, devices_all, CAPT)
    return filtered, sampled
```

```python
import jax
import jax.numpy as jnp
import ml_dtypes
import numpy as np
from jax import lax
from jax.experimental import pallas as pl
from jax.experimental.pallas import tpu as pltpu
from jax.sharding import PartitionSpec as P

GX, GY = 32, 4
DEVICES = GX * GY
PLANES = 12
ROWS, COLS = 128, 512
REACH = 8
CAP = 4
SIGMAS = (1.5, 3.0)
GROUP = 4
MESH = pl.DeviceIdType.MESH
BF16, F32 = jnp.bfloat16, jnp.float32


def make_taps():
    offsets = np.arange(2 * REACH + 1, dtype=np.float32) - np.float32(REACH)
    stacked = []
    for deviation in SIGMAS:
        profile = np.exp(-offsets * offsets / np.float32(2.0 * deviation * deviation))
        stacked.append(profile / np.sum(profile))
    return np.stack(stacked).astype(ml_dtypes.bfloat16).astype(np.float32)


def tap_lookup(taps, index):
    inside = (index >= 0) & (index <= 2 * REACH)
    return np.where(inside, taps[:, np.clip(index, 0, 2 * REACH)], 0.0)


def constant_tables():
    taps = make_taps()
    own = np.arange(ROWS)
    r = np.arange(16)
    tables = []
    for variant in range(3):
        if variant < 2:
            valid = (r // 8) == variant
            before, after = r % 8 - 8, ROWS + r % 8
        else:
            valid = np.ones(16, bool)
            before, after = r - 16, ROWS + r
        where_k = np.concatenate([own, before, after])
        keep = np.concatenate([np.ones(ROWS, bool), valid, valid])
        index = where_k[None, :] - own[:, None] + REACH
        tables.append((tap_lookup(taps, index) * keep).reshape(2 * ROWS, -1))
    along_x = np.stack(tables)
    k, n = np.arange(512)[:, None], np.arange(256)[None, :]
    along_y = tap_lookup(taps, k - 128 - n + REACH)
    plane, lane = np.arange(PLANES * 128)[:, None] // 128, np.arange(PLANES * 128)[:, None] % 128
    n = np.arange(128)[None, :]
    last = (lane >= 120) & (n == 8 * plane + lane - 120)
    first = (lane < 8) & (n == 8 * plane + lane)
    pack = np.stack([first, last]).astype(np.float32)
    unpack = np.concatenate([last.T, first.T], axis=0).astype(np.float32)
    return [np.asarray(t, np.float32).astype(ml_dtypes.bfloat16) for t in (along_x, along_y, pack, unpack)]


def hat(distance):
    return jnp.maximum(0.0, 1.0 - jnp.abs(distance))


def kernel(
    vel_hbm, ids, used, pos_hbm, bx_hbm, by_hbm, pack_hbm, unpack_hbm,
    filt_hbm, samp_ref,
    vel, pos, bx, by, pack, unpack,
    rows_first, rows_last, rows_after, rows_before,
    cols_first, cols_last, cols_after, cols_before, corners,
    halo, filt, table,
    pos_send, pos_recv, out_send, out_recv,
    in_sems, halo_send, halo_recv, pos_sems, out_sems, filt_sem,
):
    ix, iy = lax.axis_index("gx"), lax.axis_index("gy")
    me = ix * GY + iy

    loads = [
        pltpu.make_async_copy(src, dst, in_sems.at[i])
        for i, (src, dst) in enumerate(
            ((pos_hbm, pos), (vel_hbm, vel), (pack_hbm, pack), (unpack_hbm, unpack), (bx_hbm, bx), (by_hbm, by))
        )
    ]
    for load in loads:
        load.start()

    barrier = pltpu.get_barrier_semaphore()

    def device_of(number):
        return (lax.shift_right_logical(number, 2), number & (GY - 1))

    @pl.loop(1, DEVICES)
    def _(k):
        pl.semaphore_signal(barrier, 1, device_id=device_of((me + k) & (DEVICES - 1)), device_id_type=MESH)

    loads[0].wait()
    for c in range(3):
        pos_send[:, c, :] = pos[c]
    pos_send[:, 3, :] = pos[0]
    pos_recv[me] = pos_send[me]

    for load in loads[1:3]:
        load.wait()
    for pair in range(PLANES // 2):
        for buf, start, part in ((rows_first, 0, 0), (rows_last, ROWS - 16, 8)):
            low = vel[2 * pair, start : start + 16, :].astype(F32)[part : part + 8]
            high = vel[2 * pair + 1, start : start + 16, :].astype(F32)[part : part + 8]
            buf[pair] = jnp.concatenate([low, high], axis=0).astype(BF16)
    for buf, side, start in ((cols_first, 0, 0), (cols_last, 1, COLS - 128)):
        edge = jnp.concatenate([vel[p, :, start : start + 128] for p in range(PLANES)], axis=1)
        buf[...] = jnp.dot(edge, pack[side], preferred_element_type=F32).astype(BF16)

    pl.semaphore_wait(barrier, DEVICES - 1)

    x_next, x_prev = (ix + 1) & (GX - 1), (ix + GX - 1) & (GX - 1)
    y_next, y_prev = (iy + 1) & (GY - 1), (iy + GY - 1) & (GY - 1)
    top, bottom = pl.ds(0, 16), pl.ds(ROWS - 16, 16)
    halo_copies = [
        pltpu.make_async_remote_copy(
            src, dst, halo_send.at[i], halo_recv.at[i], device_id=target, device_id_type=MESH
        )
        for i, (src, dst, target) in enumerate(
            (
                (rows_first, rows_after, (x_prev, iy)),
                (rows_last, rows_before, (x_next, iy)),
                (cols_first, cols_after, (ix, y_prev)),
                (cols_last, cols_before, (ix, y_next)),
                (cols_last.at[bottom], corners.at[0], (x_next, y_next)),
                (cols_last.at[top], corners.at[1], (x_prev, y_next)),
                (cols_first.at[bottom], corners.at[2], (x_next, y_prev)),
                (cols_first.at[top], corners.at[3], (x_prev, y_prev)),
            )
        )
    ]
    for copy in halo_copies:
        copy.start()

    @pl.loop(1, DEVICES)
    def _(k):
        other = (me + k) & (DEVICES - 1)
        pltpu.make_async_remote_copy(
            pos_send.at[other], pos_recv.at[me], pos_sems.at[0], pos_sems.at[1],
            device_id=device_of(other), device_id_type=MESH,
        ).start()

    for load in loads[3:]:
        load.wait()
    for copy in halo_copies:
        copy.wait_recv()

    packed = jnp.concatenate(
        [
            jnp.concatenate([cols_before[...], corners[0], corners[1]], axis=0),
            jnp.concatenate([cols_after[...], corners[2], corners[3]], axis=0),
        ],
        axis=1,
    )
    for p in range(PLANES):
        lanes = pl.ds(128 * p, 128)
        spread = jnp.dot(packed, unpack[:, lanes], preferred_element_type=F32).astype(BF16)
        halo[p] = jnp.dot(bx[2], spread, preferred_element_type=F32).astype(BF16)

    @pl.loop(0, PLANES // 2)
    def _(pair):
        smooth = []
        for parity in range(2):
            tall = jnp.concatenate([vel[2 * pair + parity], rows_before[pair], rows_after[pair]], axis=0)
            smooth.append(jnp.dot(bx[parity], tall, preferred_element_type=F32).astype(BF16))
        for width in range(2):
            part = slice(width * ROWS, (width + 1) * ROWS)
            for half in range(2):
                results = []
                for parity in range(2):
                    edge = halo[2 * pair + parity, part, :]
                    inner = smooth[parity][part]
                    wide = (
                        jnp.concatenate([edge, inner[:, :384]], axis=1)
                        if half == 0
                        else jnp.concatenate([inner[:, 128:], edge], axis=1)
                    )
                    got = jnp.dot(wide, by[width], preferred_element_type=F32)
                    filt[width * PLANES + 2 * pair + parity, :, 256 * half : 256 * half + 256] = got.astype(BF16)
                    results.append(got)
                first_row = pl.multiple_of(width * PLANES * 8 + pair * 16, 16)
                for block_row in range(ROWS // 8):
                    both = jnp.concatenate(
                        [got[8 * block_row : 8 * block_row + 8] for got in results], axis=0
                    ).astype(BF16)
                    for tile in range(2):
                        table[block_row * 4 + half * 2 + tile, pl.ds(first_row, 16), :] = both[
                            :, 128 * tile : 128 * tile + 128
                        ]

    store = pltpu.make_async_copy(filt, filt_hbm, filt_sem)
    store.start()

    others = pl.ds(0, DEVICES - 1)
    pltpu.make_async_remote_copy(
        pos_send.at[others], pos_recv.at[others], pos_sems.at[0], pos_sems.at[1],
        device_id=(x_next, iy), device_id_type=MESH,
    ).wait()

    lane_slot = lax.shift_right_logical(lax.broadcasted_iota(jnp.int32, (1, 128), 1), 5)
    rows128 = lax.broadcasted_iota(jnp.int32, (128, 128), 0).astype(F32)
    rows8 = lax.broadcasted_iota(jnp.int32, (8, 128), 0).astype(F32)

    def sample(owner):
        numbers = [ids[q, owner] for q in range(CAP)]
        blocks = jnp.concatenate([table[lax.shift_right_logical(n, 4)] for n in numbers], axis=1)
        place = [(n & 15) * 8 for n in numbers]
        offset = jnp.where(
            lane_slot < 2,
            jnp.where(lane_slot == 0, place[0], place[1]),
            jnp.where(lane_slot == 2, place[2], place[3]),
        ).astype(F32)
        spot = pos_recv[owner]
        along_x, along_y, along_z = 7.0 * spot[0:1], 7.0 * spot[1:2], 3.0 * spot[2:3]
        target = jnp.where(lane_slot < used[0, owner], offset + along_y, -1000.0)
        weights = jnp.concatenate(
            [hat(rows128 - jnp.where(lane_slot == q, target, -1000.0)).astype(BF16) for q in range(CAP)], axis=0
        )
        picked = jnp.dot(blocks, weights, preferred_element_type=F32).reshape(6, 4, 8, 128)
        weight_x = hat(rows8 - along_x)
        total = picked[:, 0] * (weight_x * hat(along_z))
        for z in range(1, 4):
            total = total + picked[:, z] * (weight_x * hat(along_z - float(z)))
        out_send[owner] = jnp.sum(total, axis=1)

    def reply(owner):
        pltpu.make_async_remote_copy(
            out_send.at[owner], out_recv.at[me], out_sems.at[0], out_sems.at[1],
            device_id=device_of(owner), device_id_type=MESH,
        ).start()

    first = [(me + k) & (DEVICES - 1) for k in range(GROUP)]
    for owner in first:
        sample(owner)
    for owner in first[1:]:
        reply(owner)
    out_recv[me] = out_send[me]

    @pl.loop(1, DEVICES // GROUP)
    def _(group):
        owners = [(me + group * GROUP + k) & (DEVICES - 1) for k in range(GROUP)]
        for owner in owners:
            sample(owner)
        for owner in owners:
            reply(owner)

    store.wait()
    for copy in halo_copies:
        copy.wait_send()
    pltpu.make_async_remote_copy(
        out_send.at[others], out_recv.at[others], out_sems.at[0], out_sems.at[1],
        device_id=(x_next, iy), device_id_type=MESH,
    ).wait()
    for c in range(6):
        samp_ref[c] = out_recv[:, c, :]


def body(velocity, block_ids, counts, positions):
    tables = [jnp.asarray(t) for t in constant_tables()]
    hbm = pl.BlockSpec(memory_space=pl.ANY)
    smem = pl.BlockSpec(memory_space=pltpu.SMEM)
    vmem = pl.BlockSpec(memory_space=pltpu.VMEM)
    filtered, sampled = pl.pallas_call(
        kernel,
        out_shape=(
            jax.ShapeDtypeStruct((2 * PLANES, ROWS, COLS), BF16),
            jax.ShapeDtypeStruct((6, DEVICES, 128), F32),
        ),
        in_specs=[hbm, smem, smem, hbm, hbm, hbm, hbm, hbm],
        out_specs=(hbm, vmem),
        scratch_shapes=[
            pltpu.VMEM((PLANES, ROWS, COLS), BF16),
            pltpu.VMEM((3, DEVICES, 128), F32),
            *[pltpu.VMEM(t.shape, BF16) for t in tables],
            *[pltpu.VMEM((PLANES // 2, 16, COLS), BF16)] * 4,
            *[pltpu.VMEM((ROWS, 128), BF16)] * 4,
            pltpu.VMEM((4, 16, 128), BF16),
            pltpu.VMEM((PLANES, 2 * ROWS, 128), BF16),
            pltpu.VMEM((2 * PLANES, ROWS, COLS), BF16),
            pltpu.VMEM((64, 192, 128), BF16),
            pltpu.VMEM((DEVICES, 4, 128), F32),
            pltpu.VMEM((DEVICES, 4, 128), F32),
            pltpu.VMEM((DEVICES, 6, 128), F32),
            pltpu.VMEM((DEVICES, 6, 128), F32),
            pltpu.SemaphoreType.DMA((6,)),
            pltpu.SemaphoreType.DMA((8,)),
            pltpu.SemaphoreType.DMA((8,)),
            pltpu.SemaphoreType.DMA((2,)),
            pltpu.SemaphoreType.DMA((2,)),
            pltpu.SemaphoreType.DMA,
        ],
        compiler_params=pltpu.CompilerParams(
            collective_id=0, has_side_effects=True, vmem_limit_bytes=63 * 1024 * 1024
        ),
        name="filter_and_sample",
    )(
        velocity.reshape(PLANES, ROWS, COLS),
        block_ids.reshape(DEVICES, CAP).T,
        counts.reshape(1, DEVICES),
        positions.reshape(3, DEVICES, 128),
        *tables,
    )
    return filtered.reshape(2, 3, 4, ROWS, COLS), sampled.reshape(2, 3, 1, 1, DEVICES, 128)


def solution(mesh):
    return jax.shard_map(
        body,
        mesh=mesh,
        in_specs=(
            P(None, None, "gx", "gy"),
            P("gx", "gy", None, None),
            P("gx", "gy", None),
            P(None, "gx", "gy", None, None),
        ),
        out_specs=(P(None, None, None, "gx", "gy"), P(None, None, "gx", "gy", None, None)),
        check_vma=False,
    )
```

```python
import jax
import jax.numpy as jnp
import ml_dtypes
import numpy as np
from jax import lax
from jax.experimental import pallas as pl
from jax.experimental.pallas import tpu as pltpu
from jax.sharding import PartitionSpec as P

GX, GY = 32, 4
DEVICES = GX * GY
PLANES = 12
ROWS, COLS = 128, 512
REACH = 8
CAP = 4
SIGMAS = (1.5, 3.0)
GROUP = 4
BATCH = 16
TURN = 8
MESH = pl.DeviceIdType.MESH
BF16, F32 = jnp.bfloat16, jnp.float32


def make_taps():
    offsets = np.arange(2 * REACH + 1, dtype=np.float32) - np.float32(REACH)
    stacked = []
    for deviation in SIGMAS:
        profile = np.exp(-offsets * offsets / np.float32(2.0 * deviation * deviation))
        stacked.append(profile / np.sum(profile))
    return np.stack(stacked).astype(ml_dtypes.bfloat16).astype(np.float32)


def tap_lookup(taps, index):
    inside = (index >= 0) & (index <= 2 * REACH)
    return np.where(inside, taps[:, np.clip(index, 0, 2 * REACH)], 0.0)


def constant_tables():
    taps = make_taps()
    own = np.arange(ROWS)
    r = np.arange(16)
    tables = []
    for variant in range(3):
        if variant < 2:
            valid = (r // 8) == variant
            before, after = r % 8 - 8, ROWS + r % 8
        else:
            valid = np.ones(16, bool)
            before, after = r - 16, ROWS + r
        where_k = np.concatenate([own, before, after])
        keep = np.concatenate([np.ones(ROWS, bool), valid, valid])
        index = where_k[None, :] - own[:, None] + REACH
        tables.append((tap_lookup(taps, index) * keep).reshape(2 * ROWS, -1))
    along_x = np.stack(tables)
    k, n = np.arange(512)[:, None], np.arange(256)[None, :]
    along_y = tap_lookup(taps, k - 128 - n + REACH)
    plane, lane = np.arange(PLANES * 128)[:, None] // 128, np.arange(PLANES * 128)[:, None] % 128
    n = np.arange(128)[None, :]
    last = (lane >= 120) & (n == 8 * plane + lane - 120)
    first = (lane < 8) & (n == 8 * plane + lane)
    pack = np.stack([first, last]).astype(np.float32)
    unpack = np.concatenate([last.T, first.T], axis=0).astype(np.float32)
    return [np.asarray(t, np.float32).astype(ml_dtypes.bfloat16) for t in (along_x, along_y, pack, unpack)]


def hat(distance):
    return jnp.maximum(0.0, 1.0 - jnp.abs(distance))


def kernel(
    vel_hbm, ids, used, pos_hbm, bx_hbm, by_hbm, pack_hbm, unpack_hbm,
    filt, samp_ref,
    vel, pos, bx, by, pack, unpack,
    rows_first, rows_last, rows_after, rows_before,
    cols_first, cols_last, cols_after, cols_before, corners,
    halo, table, blocks,
    pos_send, pos_recv, out_send, out_recv,
    in_sems, halo_send, halo_recv, pos_sems, out_sems,
):
    ix, iy = lax.axis_index("gx"), lax.axis_index("gy")
    me = ix * GY + iy

    loads = [
        pltpu.make_async_copy(src, dst, in_sems.at[i])
        for i, (src, dst) in enumerate(
            ((pos_hbm, pos), (vel_hbm, vel), (pack_hbm, pack), (unpack_hbm, unpack), (bx_hbm, bx), (by_hbm, by))
        )
    ]
    for load in loads:
        load.start()

    barrier = pltpu.get_barrier_semaphore()

    def device_of(number):
        return (lax.shift_right_logical(number, 2), number & (GY - 1))

    @pl.loop(1, DEVICES)
    def _(k):
        pl.semaphore_signal(barrier, 1, device_id=device_of((me + k) & (DEVICES - 1)), device_id_type=MESH)

    loads[0].wait()
    for c in range(3):
        pos_send[:, c, :] = pos[c]
    pos_send[:, 3, :] = pos[0]
    pos_recv[me] = pos_send[me]

    for load in loads[1:3]:
        load.wait()
    for pair in range(PLANES // 2):
        for buf, start, part in ((rows_first, 0, 0), (rows_last, ROWS - 16, 8)):
            low = vel[2 * pair, start : start + 16, :].astype(F32)[part : part + 8]
            high = vel[2 * pair + 1, start : start + 16, :].astype(F32)[part : part + 8]
            buf[pair] = jnp.concatenate([low, high], axis=0).astype(BF16)
    for buf, side, start in ((cols_first, 0, 0), (cols_last, 1, COLS - 128)):
        edge = jnp.concatenate([vel[p, :, start : start + 128] for p in range(PLANES)], axis=1)
        buf[...] = jnp.dot(edge, pack[side], preferred_element_type=F32).astype(BF16)

    pl.semaphore_wait(barrier, DEVICES - 1)

    x_next, x_prev = (ix + 1) & (GX - 1), (ix + GX - 1) & (GX - 1)
    y_next, y_prev = (iy + 1) & (GY - 1), (iy + GY - 1) & (GY - 1)
    top, bottom = pl.ds(0, 16), pl.ds(ROWS - 16, 16)
    halo_copies = [
        pltpu.make_async_remote_copy(
            src, dst, halo_send.at[i], halo_recv.at[i], device_id=target, device_id_type=MESH
        )
        for i, (src, dst, target) in enumerate(
            (
                (rows_first, rows_after, (x_prev, iy)),
                (rows_last, rows_before, (x_next, iy)),
                (cols_first, cols_after, (ix, y_prev)),
                (cols_last, cols_before, (ix, y_next)),
                (cols_last.at[bottom], corners.at[0], (x_next, y_next)),
                (cols_last.at[top], corners.at[1], (x_prev, y_next)),
                (cols_first.at[bottom], corners.at[2], (x_next, y_prev)),
                (cols_first.at[top], corners.at[3], (x_prev, y_prev)),
            )
        )
    ]
    for copy in halo_copies:
        copy.start()

    @pl.loop(1, DEVICES)
    def _(k):
        other = (me + k) & (DEVICES - 1)
        pltpu.make_async_remote_copy(
            pos_send.at[other], pos_recv.at[me], pos_sems.at[0], pos_sems.at[1],
            device_id=device_of(other), device_id_type=MESH,
        ).start()

    for load in loads[3:]:
        load.wait()
    for copy in halo_copies:
        copy.wait_recv()

    packed = jnp.concatenate(
        [
            jnp.concatenate([cols_before[...], corners[0], corners[1]], axis=0),
            jnp.concatenate([cols_after[...], corners[2], corners[3]], axis=0),
        ],
        axis=1,
    )
    for p in range(PLANES):
        lanes = pl.ds(128 * p, 128)
        spread = jnp.dot(packed, unpack[:, lanes], preferred_element_type=F32).astype(BF16)
        halo[p] = jnp.dot(bx[2], spread, preferred_element_type=F32).astype(BF16)

    @pl.loop(0, PLANES // 2)
    def _(pair):
        smooth = []
        for parity in range(2):
            tall = jnp.concatenate([vel[2 * pair + parity], rows_before[pair], rows_after[pair]], axis=0)
            smooth.append(jnp.dot(bx[parity], tall, preferred_element_type=F32).astype(BF16))
        for width in range(2):
            part = slice(width * ROWS, (width + 1) * ROWS)
            for half in range(2):
                results = []
                for parity in range(2):
                    edge = halo[2 * pair + parity, part, :]
                    inner = smooth[parity][part]
                    wide = (
                        jnp.concatenate([edge, inner[:, :384]], axis=1)
                        if half == 0
                        else jnp.concatenate([inner[:, 128:], edge], axis=1)
                    )
                    got = jnp.dot(wide, by[width], preferred_element_type=F32)
                    filt[width * PLANES + 2 * pair + parity, :, 256 * half : 256 * half + 256] = got.astype(BF16)
                    results.append(got)
                for block_row in range(ROWS // 8):
                    both = jnp.concatenate(
                        [got[8 * block_row : 8 * block_row + 8] for got in results], axis=0
                    ).astype(BF16)
                    for tile in range(2):
                        table[block_row * 4 + half * 2 + tile, width * (PLANES // 2) + pair] = both[
                            :, 128 * tile : 128 * tile + 128
                        ]


    square = lambda axis: lax.broadcasted_iota(jnp.int32, (128, 128), axis)
    unit = jnp.where(square(0) == square(1), 1.0, 0.0).astype(BF16)

    @pl.loop(0, 64 // TURN)
    def _(step):
        for part in range(TURN):
            tile = step * TURN + part
            turned = lax.dot_general(
                unit, table[tile].reshape(192, 128), (((1,), (1,)), ((), ())), preferred_element_type=F32
            )
            blocks[pl.ds(tile * 16, 16)] = turned.reshape(16, 8, 192)

    others = pl.ds(0, DEVICES - 1)
    pltpu.make_async_remote_copy(
        pos_send.at[others], pos_recv.at[others], pos_sems.at[0], pos_sems.at[1],
        device_id=(x_next, iy), device_id_type=MESH,
    ).wait()

    lane_slot = lax.shift_right_logical(lax.broadcasted_iota(jnp.int32, (1, 128), 1), 5)
    rows8 = lax.broadcasted_iota(jnp.int32, (8, 128), 0).astype(F32)
    empty = jnp.zeros((32, 128), BF16)

    def sample(owners):
        weights = []
        listed = [blocks[ids[q, owner]] for owner in owners for q in range(CAP)]
        for u, owner in enumerate(owners):
            spot = pos_recv[owner]
            weight_y = jnp.where(lane_slot < used[0, owner], hat(rows8 - 7.0 * spot[1:2]), 0.0)
            mine = jnp.concatenate(
                [jnp.where(lane_slot == q, weight_y, 0.0) for q in range(CAP)], axis=0
            ).astype(BF16)
            weights.append(jnp.concatenate([mine if v == u else empty for v in range(GROUP)], axis=0))
        picked = lax.dot_general(
            jnp.concatenate(listed, axis=0).astype(BF16),
            jnp.concatenate(weights, axis=1),
            (((0,), (0,)), ((), ())),
            preferred_element_type=F32,
        )
        for u, owner in enumerate(owners):
            spot = pos_recv[owner]
            along_x, along_z = 7.0 * spot[0:1], 3.0 * spot[2:3]
            mine = picked[:, 128 * u : 128 * u + 128].reshape(6, 4, 8, 128)
            weight_x = hat(rows8 - along_x)
            total = mine[:, 0] * (weight_x * hat(along_z))
            for z in range(1, 4):
                total = total + mine[:, z] * (weight_x * hat(along_z - float(z)))
            out_send[owner] = jnp.sum(total, axis=1)

    def reply(owner):
        pltpu.make_async_remote_copy(
            out_send.at[owner], out_recv.at[me], out_sems.at[0], out_sems.at[1],
            device_id=device_of(owner), device_id_type=MESH,
        ).start()

    def batch(number):
        return [(me + 1 + number * BATCH + k) & (DEVICES - 1) for k in range(BATCH)]

    def sample_batch(owners):
        for start in range(0, BATCH, GROUP):
            sample(owners[start : start + GROUP])

    batches = DEVICES // BATCH

    @pl.loop(0, batches - 1)
    def _(number):
        owners = batch(number)
        sample_batch(owners)
        for owner in owners:
            reply(owner)

    owners = batch(batches - 1)
    sample_batch(owners)
    for owner in owners[:-1]:
        reply(owner)
    out_recv[me] = out_send[me]

    for copy in halo_copies:
        copy.wait_send()
    pltpu.make_async_remote_copy(
        out_send.at[others], out_recv.at[others], out_sems.at[0], out_sems.at[1],
        device_id=(x_next, iy), device_id_type=MESH,
    ).wait()
    for c in range(6):
        samp_ref[c] = out_recv[:, c, :]


def body(velocity, block_ids, counts, positions):
    tables = [jnp.asarray(t) for t in constant_tables()]
    hbm = pl.BlockSpec(memory_space=pl.ANY)
    fixed = pl.BlockSpec(memory_space=pltpu.HBM)
    smem = pl.BlockSpec(memory_space=pltpu.SMEM)
    vmem = pl.BlockSpec(memory_space=pltpu.VMEM)
    filtered, sampled = pl.pallas_call(
        kernel,
        out_shape=(
            pltpu.VMEM((2 * PLANES, ROWS, COLS), BF16),
            pltpu.VMEM((6, DEVICES, 128), F32),
        ),
        in_specs=[fixed, smem, smem, fixed, fixed, fixed, fixed, fixed],
        out_specs=(vmem, vmem),
        scratch_shapes=[
            pltpu.VMEM((PLANES, ROWS, COLS), BF16),
            pltpu.VMEM((3, DEVICES, 128), F32),
            *[pltpu.VMEM(t.shape, BF16) for t in tables],
            *[pltpu.VMEM((PLANES // 2, 16, COLS), BF16)] * 4,
            *[pltpu.VMEM((ROWS, 128), BF16)] * 4,
            pltpu.VMEM((4, 16, 128), BF16),
            pltpu.VMEM((PLANES, 2 * ROWS, 128), BF16),
            pltpu.VMEM((64, 12, 16, 128), BF16),
            pltpu.VMEM((1024, 8, 192), F32),
            pltpu.VMEM((DEVICES, 4, 128), F32),
            pltpu.VMEM((DEVICES, 4, 128), F32),
            pltpu.VMEM((DEVICES, 6, 128), F32),
            pltpu.VMEM((DEVICES, 6, 128), F32),
            pltpu.SemaphoreType.DMA((6,)),
            pltpu.SemaphoreType.DMA((8,)),
            pltpu.SemaphoreType.DMA((8,)),
            pltpu.SemaphoreType.DMA((2,)),
            pltpu.SemaphoreType.DMA((2,)),
        ],
        compiler_params=pltpu.CompilerParams(
            collective_id=0, has_side_effects=True, vmem_limit_bytes=60 * 1024 * 1024
        ),
        name="filter_and_sample",
    )(
        velocity.reshape(PLANES, ROWS, COLS),
        block_ids.reshape(DEVICES, CAP).T,
        counts.reshape(1, DEVICES),
        positions.reshape(3, DEVICES, 128),
        *tables,
    )
    return filtered.reshape(2, 3, 4, ROWS, COLS), sampled.reshape(2, 3, 1, 1, DEVICES, 128)


def solution(mesh):
    return jax.shard_map(
        body,
        mesh=mesh,
        in_specs=(
            P(None, None, "gx", "gy"),
            P("gx", "gy", None, None),
            P("gx", "gy", None),
            P(None, "gx", "gy", None, None),
        ),
        out_specs=(P(None, None, None, "gx", "gy"), P(None, None, "gx", "gy", None, None)),
        check_vma=False,
    )
```

```python
import jax
import jax.numpy as jnp
import ml_dtypes
import numpy as np
from jax import lax
from jax.experimental import pallas as pl
from jax.experimental.pallas import tpu as pltpu
from jax.sharding import PartitionSpec as P

GX, GY = 32, 4
DEVICES = GX * GY
PLANES = 12
ROWS, COLS = 128, 512
REACH = 8
CAP = 4
SIGMAS = (1.5, 3.0)
GROUP = 4
BATCH = 16
TURN = 16
MESH, LOGICAL = pl.DeviceIdType.MESH, pl.DeviceIdType.LOGICAL
BF16, F32 = jnp.bfloat16, jnp.float32


def make_taps():
    offsets = np.arange(2 * REACH + 1, dtype=np.float32) - np.float32(REACH)
    stacked = []
    for deviation in SIGMAS:
        profile = np.exp(-offsets * offsets / np.float32(2.0 * deviation * deviation))
        stacked.append(profile / np.sum(profile))
    return np.stack(stacked).astype(ml_dtypes.bfloat16).astype(np.float32)


def tap_lookup(taps, index):
    inside = (index >= 0) & (index <= 2 * REACH)
    return np.where(inside, taps[:, np.clip(index, 0, 2 * REACH)], 0.0)


def constant_tables():
    taps = make_taps()
    own = np.arange(ROWS)
    r = np.arange(16)
    tables = []
    for variant in range(3):
        if variant < 2:
            valid = (r // 8) == variant
            before, after = r % 8 - 8, ROWS + r % 8
        else:
            valid = np.ones(16, bool)
            before, after = r - 16, ROWS + r
        where_k = np.concatenate([own, before, after])
        keep = np.concatenate([np.ones(ROWS, bool), valid, valid])
        index = where_k[None, :] - own[:, None] + REACH
        tables.append((tap_lookup(taps, index) * keep).reshape(2 * ROWS, -1))
    along_x = np.stack(tables)
    k, n = np.arange(512)[:, None], np.arange(256)[None, :]
    along_y = tap_lookup(taps, k - 128 - n + REACH)
    plane, lane = np.arange(PLANES * 128)[:, None] // 128, np.arange(PLANES * 128)[:, None] % 128
    n = np.arange(128)[None, :]
    last = (lane >= 120) & (n == 8 * plane + lane - 120)
    first = (lane < 8) & (n == 8 * plane + lane)
    pack = np.stack([first, last]).astype(np.float32)
    unpack = np.concatenate([last.T, first.T], axis=0).astype(np.float32)
    return [np.asarray(t, np.float32).astype(ml_dtypes.bfloat16) for t in (along_x, along_y, pack, unpack)]


def hat(distance):
    return jnp.maximum(0.0, 1.0 - jnp.abs(distance))


def kernel(
    vel_hbm, ids, used, pos_hbm, bx_hbm, by_hbm, pack_hbm, unpack_hbm,
    filt, out_recv,
    vel, pos, bx, by, pack, unpack,
    rows_first, rows_last, rows_after, rows_before,
    cols_first, cols_last, cols_after, cols_before, corners,
    table, blocks,
    pos_send, pos_recv, out_send,
    in_sems, halo_send, halo_recv, pos_sems, out_sems,
):
    ix, iy = lax.axis_index("gx"), lax.axis_index("gy")
    me = ix * GY + iy

    loads = [
        pltpu.make_async_copy(src, dst, in_sems.at[i])
        for i, (src, dst) in enumerate(
            ((pos_hbm, pos), (vel_hbm, vel), (pack_hbm, pack), (unpack_hbm, unpack), (bx_hbm, bx), (by_hbm, by))
        )
    ]
    for load in loads:
        load.start()

    barrier = pltpu.get_barrier_semaphore()

    def device_of(number):
        return number

    def greet(distance):
        pl.semaphore_signal(
            barrier, 1, device_id=device_of((me + distance) & (DEVICES - 1)), device_id_type=LOGICAL
        )

    for near in range(1, 10):
        greet(near)
        greet(DEVICES - near)

    @pl.loop(1, 7)
    def _(step):
        for near in range(1, 10):
            greet(step * 9 + near)
            greet(DEVICES - step * 9 - near)

    greet(DEVICES // 2)

    loads[0].wait()
    for c in range(3):
        pos_send[:, c, :] = pos[c]
    pos_send[:, 3, :] = pos[0]
    pos_recv[me] = pos_send[me]

    for load in loads[1:3]:
        load.wait()
    for pair in range(PLANES // 2):
        for buf, start, part in ((rows_first, 0, 0), (rows_last, ROWS - 16, 8)):
            low = vel[2 * pair, start : start + 16, :].astype(F32)[part : part + 8]
            high = vel[2 * pair + 1, start : start + 16, :].astype(F32)[part : part + 8]
            buf[pair] = jnp.concatenate([low, high], axis=0).astype(BF16)
    for buf, side, start in ((cols_first, 0, 0), (cols_last, 1, COLS - 128)):
        edge = jnp.concatenate([vel[p, :, start : start + 128] for p in range(PLANES)], axis=1)
        buf[...] = jnp.dot(edge, pack[side], preferred_element_type=F32).astype(BF16)

    pl.semaphore_wait(barrier, DEVICES - 1)

    x_next, x_prev = (ix + 1) & (GX - 1), (ix + GX - 1) & (GX - 1)
    y_next, y_prev = (iy + 1) & (GY - 1), (iy + GY - 1) & (GY - 1)
    top, bottom = pl.ds(0, 16), pl.ds(ROWS - 16, 16)
    halo_copies = [
        pltpu.make_async_remote_copy(
            src, dst, halo_send.at[i], halo_recv.at[i], device_id=target, device_id_type=MESH
        )
        for i, (src, dst, target) in enumerate(
            (
                (rows_first, rows_after, (x_prev, iy)),
                (rows_last, rows_before, (x_next, iy)),
                (cols_first, cols_after, (ix, y_prev)),
                (cols_last, cols_before, (ix, y_next)),
                (cols_last.at[bottom], corners.at[0], (x_next, y_next)),
                (cols_last.at[top], corners.at[1], (x_prev, y_next)),
                (cols_first.at[bottom], corners.at[2], (x_next, y_prev)),
                (cols_first.at[top], corners.at[3], (x_prev, y_prev)),
            )
        )
    ]
    for copy in halo_copies:
        copy.start()

    def send_place(distance):
        other = (me + distance) & (DEVICES - 1)
        pltpu.make_async_remote_copy(
            pos_send.at[other], pos_recv.at[me], pos_sems.at[0], pos_sems.at[1],
            device_id=device_of(other), device_id_type=LOGICAL,
        ).start()

    send_place(DEVICES // 2)

    @pl.loop(0, 7)
    def _(step):
        for near in range(1, 10):
            send_place(step * 9 + near)
            send_place(DEVICES - step * 9 - near)

    for load in loads[3:]:
        load.wait()
    for copy in halo_copies:
        copy.wait_recv()

    packed = jnp.concatenate(
        [
            jnp.concatenate([cols_before[...], corners[0], corners[1]], axis=0),
            jnp.concatenate([cols_after[...], corners[2], corners[3]], axis=0),
        ],
        axis=1,
    )
    aside = jnp.dot(bx[2], packed, preferred_element_type=F32).astype(BF16)

    @pl.loop(0, PLANES // 2)
    def _(pair):
        lanes = pl.ds(pl.multiple_of(256 * pair, 256), 256)
        edges = jnp.dot(aside, unpack[:, lanes], preferred_element_type=F32).astype(BF16)
        smooth = []
        for parity in range(2):
            tall = jnp.concatenate([vel[2 * pair + parity], rows_before[pair], rows_after[pair]], axis=0)
            smooth.append(jnp.dot(bx[parity], tall, preferred_element_type=F32).astype(BF16))
        for width in range(2):
            part = slice(width * ROWS, (width + 1) * ROWS)
            for half in range(2):
                results = []
                for parity in range(2):
                    edge = edges[part, 128 * parity : 128 * parity + 128]
                    inner = smooth[parity][part]
                    wide = (
                        jnp.concatenate([edge, inner[:, :384]], axis=1)
                        if half == 0
                        else jnp.concatenate([inner[:, 128:], edge], axis=1)
                    )
                    got = jnp.dot(wide, by[width], preferred_element_type=F32)
                    filt[width * PLANES + 2 * pair + parity, :, 256 * half : 256 * half + 256] = got.astype(BF16)
                    results.append(got)
                for block_row in range(ROWS // 8):
                    both = jnp.concatenate(
                        [got[8 * block_row : 8 * block_row + 8] for got in results], axis=0
                    ).astype(BF16)
                    for tile in range(2):
                        table[block_row * 4 + half * 2 + tile, width * (PLANES // 2) + pair] = both[
                            :, 128 * tile : 128 * tile + 128
                        ]


    square = lambda axis: lax.broadcasted_iota(jnp.int32, (128, 128), axis)
    unit = jnp.where(square(0) == square(1), 1.0, 0.0).astype(BF16)

    @pl.loop(0, 64 // TURN)
    def _(step):
        for part in range(TURN):
            tile = step * TURN + part
            if True:
                turned = table[tile].reshape(192, 128).T.astype(F32)
            else:
                turned = lax.dot_general(
                    unit, table[tile].reshape(192, 128), (((1,), (1,)), ((), ())), preferred_element_type=F32
                )
            blocks[pl.ds(tile * 16, 16)] = turned.reshape(16, 8, 192)

    others = pl.ds(0, DEVICES - 1)
    pltpu.make_async_remote_copy(
        pos_send.at[others], pos_recv.at[others], pos_sems.at[0], pos_sems.at[1],
        device_id=(x_next, iy), device_id_type=MESH,
    ).wait()

    lane_slot = lax.shift_right_logical(lax.broadcasted_iota(jnp.int32, (1, 128), 1), 5)
    rows8 = lax.broadcasted_iota(jnp.int32, (8, 128), 0).astype(F32)
    empty = jnp.zeros((32, 128), BF16)

    def sample(owners):
        weights = []
        listed = [blocks[ids[q, owner]] for owner in owners for q in range(CAP)]
        for u, owner in enumerate(owners):
            spot = pos_recv[owner]
            weight_y = jnp.where(lane_slot < used[0, owner], hat(rows8 - 7.0 * spot[1:2]), 0.0)
            mine = jnp.concatenate(
                [jnp.where(lane_slot == q, weight_y, 0.0) for q in range(CAP)], axis=0
            ).astype(BF16)
            weights.append(jnp.concatenate([mine if v == u else empty for v in range(GROUP)], axis=0))
        picked = lax.dot_general(
            jnp.concatenate(listed, axis=0).astype(BF16),
            jnp.concatenate(weights, axis=1),
            (((0,), (0,)), ((), ())),
            preferred_element_type=F32,
        )
        for u, owner in enumerate(owners):
            spot = pos_recv[owner]
            along_x, along_z = 7.0 * spot[0:1], 3.0 * spot[2:3]
            mine = picked[:, 128 * u : 128 * u + 128].reshape(6, 4, 8, 128)
            weight_x = hat(rows8 - along_x)
            total = mine[:, 0] * (weight_x * hat(along_z))
            for z in range(1, 4):
                total = total + mine[:, z] * (weight_x * hat(along_z - float(z)))
            out_send[owner] = jnp.sum(total, axis=1)

    def reply(owner):
        pltpu.make_async_remote_copy(
            out_send.at[owner], out_recv.at[me], out_sems.at[0], out_sems.at[1],
            device_id=device_of(owner), device_id_type=LOGICAL,
        ).start()

    def batch(number):
        return [(me + 1 + number * BATCH + k) & (DEVICES - 1) for k in range(BATCH)]

    def sample_batch(owners):
        for start in range(0, BATCH, GROUP):
            sample(owners[start : start + GROUP])

    batches = DEVICES // BATCH

    @pl.loop(0, batches - 1)
    def _(number):
        owners = batch(number)
        sample_batch(owners)
        for owner in owners:
            reply(owner)

    owners = batch(batches - 1)
    sample_batch(owners)
    for owner in owners[:-1]:
        reply(owner)
    out_recv[me] = out_send[me]

    for copy in halo_copies:
        copy.wait_send()
    pltpu.make_async_remote_copy(
        out_send.at[others], out_recv.at[others], out_sems.at[0], out_sems.at[1],
        device_id=(x_next, iy), device_id_type=MESH,
    ).wait()


def finish(filt, got, filt_out, samp_out, landed, samp, sems):
    first = pltpu.make_async_copy(got, landed, sems.at[0])
    second = pltpu.make_async_copy(filt, filt_out, sems.at[1])
    first.start()
    second.start()
    first.wait()
    for c in range(6):
        samp[c] = landed[:, c, :]
    third = pltpu.make_async_copy(samp, samp_out, sems.at[2])
    third.start()
    third.wait()
    second.wait()


def body(velocity, block_ids, counts, positions):
    tables = [jnp.asarray(t) for t in constant_tables()]
    hbm = pl.BlockSpec(memory_space=pl.ANY)
    fixed = pl.BlockSpec(memory_space=pltpu.HBM)
    smem = pl.BlockSpec(memory_space=pltpu.SMEM)
    vmem = pl.BlockSpec(memory_space=pltpu.VMEM)
    filtered, landed = pl.pallas_call(
        kernel,
        out_shape=(
            pltpu.VMEM((2 * PLANES, ROWS, COLS), BF16),
            pltpu.VMEM((DEVICES, 6, 128), F32),
        ),
        in_specs=[fixed, smem, smem, fixed, fixed, fixed, fixed, fixed],
        out_specs=(vmem, vmem),
        scratch_shapes=[
            pltpu.VMEM((PLANES, ROWS, COLS), BF16),
            pltpu.VMEM((3, DEVICES, 128), F32),
            *[pltpu.VMEM(t.shape, BF16) for t in tables],
            *[pltpu.VMEM((PLANES // 2, 16, COLS), BF16)] * 4,
            *[pltpu.VMEM((ROWS, 128), BF16)] * 4,
            pltpu.VMEM((4, 16, 128), BF16),
            pltpu.VMEM((64, 12, 16, 128), BF16),
            pltpu.VMEM((1024, 8, 192), F32),
            pltpu.VMEM((DEVICES, 4, 128), F32),
            pltpu.VMEM((DEVICES, 4, 128), F32),
            pltpu.VMEM((DEVICES, 6, 128), F32),
            pltpu.SemaphoreType.DMA((6,)),
            pltpu.SemaphoreType.DMA((8,)),
            pltpu.SemaphoreType.DMA((8,)),
            pltpu.SemaphoreType.DMA((2,)),
            pltpu.SemaphoreType.DMA((2,)),
        ],
        compiler_params=pltpu.CompilerParams(
            collective_id=0, has_side_effects=True, vmem_limit_bytes=60 * 1024 * 1024
        ),
        name="filter_and_sample",
    )(
        velocity.reshape(PLANES, ROWS, COLS),
        block_ids.reshape(DEVICES, CAP).T,
        counts.reshape(1, DEVICES),
        positions.reshape(3, DEVICES, 128),
        *tables,
    )
    filtered, sampled = pl.pallas_call(
        finish,
        out_shape=(
            jax.ShapeDtypeStruct((2 * PLANES, ROWS, COLS), BF16),
            jax.ShapeDtypeStruct((6, DEVICES, 128), F32),
        ),
        in_specs=[hbm, hbm],
        out_specs=(hbm, hbm),
        scratch_shapes=[
            pltpu.VMEM((DEVICES, 6, 128), F32),
            pltpu.VMEM((6, DEVICES, 128), F32),
            pltpu.SemaphoreType.DMA((3,)),
        ],
        compiler_params=pltpu.CompilerParams(vmem_limit_bytes=2 * 1024 * 1024),
        name="finish",
    )(filtered, landed)
    return filtered.reshape(2, 3, 4, ROWS, COLS), sampled.reshape(2, 3, 1, 1, DEVICES, 128)


def solution(mesh):
    return jax.shard_map(
        body,
        mesh=mesh,
        in_specs=(
            P(None, None, "gx", "gy"),
            P("gx", "gy", None, None),
            P("gx", "gy", None),
            P(None, "gx", "gy", None, None),
        ),
        out_specs=(P(None, None, None, "gx", "gy"), P(None, None, "gx", "gy", None, None)),
        check_vma=False,
    )
```

```python
import jax
import jax.numpy as jnp
import ml_dtypes
import numpy as np
from jax import lax
from jax.experimental import pallas as pl
from jax.experimental.pallas import tpu as pltpu
from jax.sharding import PartitionSpec as P

GX, GY = 32, 4
DEVICES = GX * GY
PLANES = 12
ROWS, COLS = 128, 512
REACH = 8
CAP = 4
SIGMAS = (1.5, 3.0)
GROUP = 4
BATCH = 16
TURN = 16
MESH, LOGICAL = pl.DeviceIdType.MESH, pl.DeviceIdType.LOGICAL
BF16, F32 = jnp.bfloat16, jnp.float32


def make_taps():
    offsets = np.arange(2 * REACH + 1, dtype=np.float32) - np.float32(REACH)
    stacked = []
    for deviation in SIGMAS:
        profile = np.exp(-offsets * offsets / np.float32(2.0 * deviation * deviation))
        stacked.append(profile / np.sum(profile))
    return np.stack(stacked).astype(ml_dtypes.bfloat16).astype(np.float32)


def tap_lookup(taps, index):
    inside = (index >= 0) & (index <= 2 * REACH)
    return np.where(inside, taps[:, np.clip(index, 0, 2 * REACH)], 0.0)


def constant_tables():
    taps = make_taps()
    own = np.arange(ROWS)
    r = np.arange(16)
    tables = []
    for variant in range(3):
        if variant < 2:
            valid = (r // 8) == variant
            before, after = r % 8 - 8, ROWS + r % 8
        else:
            valid = np.ones(16, bool)
            before, after = r - 16, ROWS + r
        where_k = np.concatenate([own, before, after])
        keep = np.concatenate([np.ones(ROWS, bool), valid, valid])
        index = where_k[None, :] - own[:, None] + REACH
        tables.append((tap_lookup(taps, index) * keep).reshape(2 * ROWS, -1))
    along_x = np.stack(tables)
    k, n = np.arange(512)[:, None], np.arange(256)[None, :]
    along_y = tap_lookup(taps, k - 128 - n + REACH)
    plane, lane = np.arange(PLANES * 128)[:, None] // 128, np.arange(PLANES * 128)[:, None] % 128
    n = np.arange(128)[None, :]
    last = (lane >= 120) & (n == 8 * plane + lane - 120)
    first = (lane < 8) & (n == 8 * plane + lane)
    pack = np.stack([first, last]).astype(np.float32)
    unpack = np.concatenate([last.T, first.T], axis=0).astype(np.float32)
    return [np.asarray(t, np.float32).astype(ml_dtypes.bfloat16) for t in (along_x, along_y, pack, unpack)]


def hat(distance):
    return jnp.maximum(0.0, 1.0 - jnp.abs(distance))


def kernel(
    vel_hbm, ids, used, pos_hbm, bx_hbm, by_hbm, pack_hbm, unpack_hbm,
    filt, out_recv,
    vel, pos, bx, by, pack, unpack,
    rows_first, rows_last, rows_after, rows_before,
    cols_first, cols_last, cols_after, cols_before, corners,
    early, table, blocks,
    pos_send, pos_recv, out_send,
    in_sems, halo_send, halo_recv, pos_sems, out_sems,
):
    ix, iy = lax.axis_index("gx"), lax.axis_index("gy")
    me = ix * GY + iy

    loads = [
        pltpu.make_async_copy(src, dst, in_sems.at[i])
        for i, (src, dst) in enumerate(
            ((pos_hbm, pos), (vel_hbm, vel), (pack_hbm, pack), (unpack_hbm, unpack), (bx_hbm, bx), (by_hbm, by))
        )
    ]
    for load in loads:
        load.start()

    barrier = pltpu.get_barrier_semaphore()

    def device_of(number):
        return number

    def greet(distance):
        pl.semaphore_signal(
            barrier, 1, device_id=device_of((me + distance) & (DEVICES - 1)), device_id_type=LOGICAL
        )

    for near in range(1, 10):
        greet(near)
        greet(DEVICES - near)

    @pl.loop(1, 7)
    def _(step):
        for near in range(1, 10):
            greet(step * 9 + near)
            greet(DEVICES - step * 9 - near)

    greet(DEVICES // 2)

    loads[0].wait()
    for c in range(3):
        pos_send[:, c, :] = pos[c]
    pos_send[:, 3, :] = pos[0]
    pos_recv[me] = pos_send[me]

    for load in loads[1:3]:
        load.wait()
    for pair in range(PLANES // 2):
        for buf, start, part in ((rows_first, 0, 0), (rows_last, ROWS - 16, 8)):
            low = vel[2 * pair, start : start + 16, :].astype(F32)[part : part + 8]
            high = vel[2 * pair + 1, start : start + 16, :].astype(F32)[part : part + 8]
            buf[pair] = jnp.concatenate([low, high], axis=0).astype(BF16)
    for buf, side, start in ((cols_first, 0, 0), (cols_last, 1, COLS - 128)):
        edge = jnp.concatenate([vel[p, :, start : start + 128] for p in range(PLANES)], axis=1)
        buf[...] = jnp.dot(edge, pack[side], preferred_element_type=F32).astype(BF16)

    pl.semaphore_wait(barrier, DEVICES - 1)

    x_next, x_prev = (ix + 1) & (GX - 1), (ix + GX - 1) & (GX - 1)
    y_next, y_prev = (iy + 1) & (GY - 1), (iy + GY - 1) & (GY - 1)
    top, bottom = pl.ds(0, 16), pl.ds(ROWS - 16, 16)
    halo_copies = [
        pltpu.make_async_remote_copy(
            src, dst, halo_send.at[i], halo_recv.at[i], device_id=target, device_id_type=MESH
        )
        for i, (src, dst, target) in enumerate(
            (
                (rows_first, rows_after, (x_prev, iy)),
                (rows_last, rows_before, (x_next, iy)),
                (cols_first, cols_after, (ix, y_prev)),
                (cols_last, cols_before, (ix, y_next)),
                (cols_last.at[bottom], corners.at[0], (x_next, y_next)),
                (cols_last.at[top], corners.at[1], (x_prev, y_next)),
                (cols_first.at[bottom], corners.at[2], (x_next, y_prev)),
                (cols_first.at[top], corners.at[3], (x_prev, y_prev)),
            )
        )
    ]
    for copy in halo_copies:
        copy.start()

    def send_place(distance):
        other = (me + distance) & (DEVICES - 1)
        pltpu.make_async_remote_copy(
            pos_send.at[other], pos_recv.at[me], pos_sems.at[0], pos_sems.at[1],
            device_id=device_of(other), device_id_type=LOGICAL,
        ).start()

    send_place(DEVICES // 2)

    @pl.loop(0, 7)
    def _(step):
        for near in range(1, 10):
            send_place(step * 9 + near)
            send_place(DEVICES - step * 9 - near)

    for load in loads[3:]:
        load.wait()

    @pl.loop(0, PLANES // 2)
    def _(pair):
        for parity in range(2):
            early[2 * pair + parity] = jnp.dot(
                bx[2, :, :ROWS], vel[2 * pair + parity], preferred_element_type=F32
            ).astype(BF16)

    for copy in halo_copies:
        copy.wait_recv()

    packed = jnp.concatenate(
        [
            jnp.concatenate([cols_before[...], corners[0], corners[1]], axis=0),
            jnp.concatenate([cols_after[...], corners[2], corners[3]], axis=0),
        ],
        axis=1,
    )
    aside = jnp.dot(bx[2], packed, preferred_element_type=F32).astype(BF16)

    @pl.loop(0, PLANES // 2)
    def _(pair):
        lanes = pl.ds(pl.multiple_of(256 * pair, 256), 256)
        edges = jnp.dot(aside, unpack[:, lanes], preferred_element_type=F32).astype(BF16)
        smooth = []
        for parity in range(2):
            tall = jnp.concatenate([vel[2 * pair + parity], rows_before[pair], rows_after[pair]], axis=0)
            ends = jnp.concatenate(
                [bx[parity, start : start + 16] for start in (0, ROWS - 16, ROWS, 2 * ROWS - 16)], axis=0
            )
            late = jnp.dot(ends, tall, preferred_element_type=F32).astype(BF16)
            smooth.append(
                [
                    jnp.concatenate(
                        [
                            late[32 * width : 32 * width + 16],
                            early[2 * pair + parity, width * ROWS + 16 : width * ROWS + ROWS - 16],
                            late[32 * width + 16 : 32 * width + 32],
                        ],
                        axis=0,
                    )
                    for width in range(2)
                ]
            )
        for width in range(2):
            part = slice(width * ROWS, (width + 1) * ROWS)
            for half in range(2):
                results = []
                for parity in range(2):
                    edge = edges[part, 128 * parity : 128 * parity + 128]
                    inner = smooth[parity][width]
                    wide = (
                        jnp.concatenate([edge, inner[:, :384]], axis=1)
                        if half == 0
                        else jnp.concatenate([inner[:, 128:], edge], axis=1)
                    )
                    got = jnp.dot(wide, by[width], preferred_element_type=F32)
                    filt[width * PLANES + 2 * pair + parity, :, 256 * half : 256 * half + 256] = got.astype(BF16)
                    results.append(got)
                for block_row in range(ROWS // 8):
                    both = jnp.concatenate(
                        [got[8 * block_row : 8 * block_row + 8] for got in results], axis=0
                    ).astype(BF16)
                    for tile in range(2):
                        table[block_row * 4 + half * 2 + tile, width * (PLANES // 2) + pair] = both[
                            :, 128 * tile : 128 * tile + 128
                        ]


    square = lambda axis: lax.broadcasted_iota(jnp.int32, (128, 128), axis)
    unit = jnp.where(square(0) == square(1), 1.0, 0.0).astype(BF16)

    @pl.loop(0, 64 // TURN)
    def _(step):
        for part in range(TURN):
            tile = step * TURN + part
            if True:
                turned = table[tile].reshape(192, 128).T.astype(F32)
            else:
                turned = lax.dot_general(
                    unit, table[tile].reshape(192, 128), (((1,), (1,)), ((), ())), preferred_element_type=F32
                )
            blocks[pl.ds(tile * 16, 16)] = turned.reshape(16, 8, 192)

    others = pl.ds(0, DEVICES - 1)
    pltpu.make_async_remote_copy(
        pos_send.at[others], pos_recv.at[others], pos_sems.at[0], pos_sems.at[1],
        device_id=(x_next, iy), device_id_type=MESH,
    ).wait()

    lane_slot = lax.shift_right_logical(lax.broadcasted_iota(jnp.int32, (1, 128), 1), 5)
    rows8 = lax.broadcasted_iota(jnp.int32, (8, 128), 0).astype(F32)
    empty = jnp.zeros((32, 128), BF16)

    def sample(owners):
        weights = []
        listed = [blocks[ids[q, owner]] for owner in owners for q in range(CAP)]
        for u, owner in enumerate(owners):
            spot = pos_recv[owner]
            weight_y = jnp.where(lane_slot < used[0, owner], hat(rows8 - 7.0 * spot[1:2]), 0.0)
            mine = jnp.concatenate(
                [jnp.where(lane_slot == q, weight_y, 0.0) for q in range(CAP)], axis=0
            ).astype(BF16)
            weights.append(jnp.concatenate([mine if v == u else empty for v in range(GROUP)], axis=0))
        picked = lax.dot_general(
            jnp.concatenate(listed, axis=0).astype(BF16),
            jnp.concatenate(weights, axis=1),
            (((0,), (0,)), ((), ())),
            preferred_element_type=F32,
        )
        for u, owner in enumerate(owners):
            spot = pos_recv[owner]
            along_x, along_z = 7.0 * spot[0:1], 3.0 * spot[2:3]
            mine = picked[:, 128 * u : 128 * u + 128].reshape(6, 4, 8, 128)
            weight_x = hat(rows8 - along_x)
            total = mine[:, 0] * (weight_x * hat(along_z))
            for z in range(1, 4):
                total = total + mine[:, z] * (weight_x * hat(along_z - float(z)))
            out_send[owner] = jnp.sum(total, axis=1)

    def reply(owner):
        pltpu.make_async_remote_copy(
            out_send.at[owner], out_recv.at[me], out_sems.at[0], out_sems.at[1],
            device_id=device_of(owner), device_id_type=LOGICAL,
        ).start()

    def batch(number):
        steps = [number * BATCH + k for k in range(BATCH)]
        codes = [
            (j & 64) | ((j & 4) << 2) | ((j & 16) >> 3) | ((j & 1) << 5) | (j & 8) | ((j & 32) >> 5) | ((j & 2) << 1)
            for j in steps
        ]
        return [me ^ (((j ^ 86) & 86) | ((j ^ (j >> 1)) & 41)) for j in codes]

    def sample_batch(owners):
        for start in range(0, BATCH, GROUP):
            sample(owners[start : start + GROUP])

    batches = DEVICES // BATCH

    @pl.loop(0, batches - 1)
    def _(number):
        owners = batch(number)
        sample_batch(owners)
        for owner in owners:
            reply(owner)

    owners = batch(batches - 1)
    sample_batch(owners)
    for owner in owners[:-1]:
        reply(owner)
    out_recv[me] = out_send[me]

    for copy in halo_copies:
        copy.wait_send()
    pltpu.make_async_remote_copy(
        out_send.at[others], out_recv.at[others], out_sems.at[0], out_sems.at[1],
        device_id=(x_next, iy), device_id_type=MESH,
    ).wait()


def finish(filt, got, filt_out, samp_out, landed, samp, sems):
    first = pltpu.make_async_copy(got, landed, sems.at[0])
    second = pltpu.make_async_copy(filt, filt_out, sems.at[1])
    first.start()
    second.start()
    first.wait()
    for c in range(6):
        samp[c] = landed[:, c, :]
    third = pltpu.make_async_copy(samp, samp_out, sems.at[2])
    third.start()
    third.wait()
    second.wait()


def body(velocity, block_ids, counts, positions):
    tables = [jnp.asarray(t) for t in constant_tables()]
    hbm = pl.BlockSpec(memory_space=pl.ANY)
    fixed = pl.BlockSpec(memory_space=pltpu.HBM)
    smem = pl.BlockSpec(memory_space=pltpu.SMEM)
    vmem = pl.BlockSpec(memory_space=pltpu.VMEM)
    filtered, landed = pl.pallas_call(
        kernel,
        out_shape=(
            pltpu.VMEM((2 * PLANES, ROWS, COLS), BF16),
            pltpu.VMEM((DEVICES, 6, 128), F32),
        ),
        in_specs=[fixed, smem, smem, fixed, fixed, fixed, fixed, fixed],
        out_specs=(vmem, vmem),
        scratch_shapes=[
            pltpu.VMEM((PLANES, ROWS, COLS), BF16),
            pltpu.VMEM((3, DEVICES, 128), F32),
            *[pltpu.VMEM(t.shape, BF16) for t in tables],
            *[pltpu.VMEM((PLANES // 2, 16, COLS), BF16)] * 4,
            *[pltpu.VMEM((ROWS, 128), BF16)] * 4,
            pltpu.VMEM((4, 16, 128), BF16),
            pltpu.VMEM((PLANES, 2 * ROWS, COLS), BF16),
            pltpu.VMEM((64, 12, 16, 128), BF16),
            pltpu.VMEM((1024, 8, 192), F32),
            pltpu.VMEM((DEVICES, 4, 128), F32),
            pltpu.VMEM((DEVICES, 4, 128), F32),
            pltpu.VMEM((DEVICES, 6, 128), F32),
            pltpu.SemaphoreType.DMA((6,)),
            pltpu.SemaphoreType.DMA((8,)),
            pltpu.SemaphoreType.DMA((8,)),
            pltpu.SemaphoreType.DMA((2,)),
            pltpu.SemaphoreType.DMA((2,)),
        ],
        compiler_params=pltpu.CompilerParams(
            collective_id=0, has_side_effects=True, vmem_limit_bytes=60 * 1024 * 1024
        ),
        name="filter_and_sample",
    )(
        velocity.reshape(PLANES, ROWS, COLS),
        block_ids.reshape(DEVICES, CAP).T,
        counts.reshape(1, DEVICES),
        positions.reshape(3, DEVICES, 128),
        *tables,
    )
    filtered, sampled = pl.pallas_call(
        finish,
        out_shape=(
            jax.ShapeDtypeStruct((2 * PLANES, ROWS, COLS), BF16),
            jax.ShapeDtypeStruct((6, DEVICES, 128), F32),
        ),
        in_specs=[hbm, hbm],
        out_specs=(hbm, hbm),
        scratch_shapes=[
            pltpu.VMEM((DEVICES, 6, 128), F32),
            pltpu.VMEM((6, DEVICES, 128), F32),
            pltpu.SemaphoreType.DMA((3,)),
        ],
        compiler_params=pltpu.CompilerParams(vmem_limit_bytes=2 * 1024 * 1024),
        name="finish",
    )(filtered, landed)
    return filtered.reshape(2, 3, 4, ROWS, COLS), sampled.reshape(2, 3, 1, 1, DEVICES, 128)


def solution(mesh):
    return jax.shard_map(
        body,
        mesh=mesh,
        in_specs=(
            P(None, None, "gx", "gy"),
            P("gx", "gy", None, None),
            P("gx", "gy", None),
            P(None, "gx", "gy", None, None),
        ),
        out_specs=(P(None, None, None, "gx", "gy"), P(None, None, "gx", "gy", None, None)),
        check_vma=False,
    )
```

```python
import jax
import jax.numpy as jnp
import ml_dtypes
import numpy as np
from jax import lax
from jax.experimental import pallas as pl
from jax.experimental.pallas import tpu as pltpu
from jax.sharding import PartitionSpec as P

GX, GY = 32, 4
DEVICES = GX * GY
PLANES = 12
ROWS, COLS = 128, 512
REACH = 8
CAP = 4
SIGMAS = (1.5, 3.0)
GROUP = 4
BATCH = 32
TURN = 16
MESH, LOGICAL = pl.DeviceIdType.MESH, pl.DeviceIdType.LOGICAL
BF16, F32 = jnp.bfloat16, jnp.float32


def make_taps():
    offsets = np.arange(2 * REACH + 1, dtype=np.float32) - np.float32(REACH)
    stacked = []
    for deviation in SIGMAS:
        profile = np.exp(-offsets * offsets / np.float32(2.0 * deviation * deviation))
        stacked.append(profile / np.sum(profile))
    return np.stack(stacked).astype(ml_dtypes.bfloat16).astype(np.float32)


def tap_lookup(taps, index):
    inside = (index >= 0) & (index <= 2 * REACH)
    return np.where(inside, taps[:, np.clip(index, 0, 2 * REACH)], 0.0)


def constant_tables():
    taps = make_taps()
    own = np.arange(ROWS)
    r = np.arange(16)
    tables = []
    for variant in range(3):
        if variant < 2:
            valid = (r // 8) == variant
            before, after = r % 8 - 8, ROWS + r % 8
        else:
            valid = np.ones(16, bool)
            before, after = r - 16, ROWS + r
        where_k = np.concatenate([own, before, after])
        keep = np.concatenate([np.ones(ROWS, bool), valid, valid])
        index = where_k[None, :] - own[:, None] + REACH
        tables.append((tap_lookup(taps, index) * keep).reshape(2 * ROWS, -1))
    along_x = np.stack(tables)
    k, n = np.arange(512)[:, None], np.arange(256)[None, :]
    along_y = tap_lookup(taps, k - 128 - n + REACH)
    edge_y = np.concatenate([along_y[:, :128, :128] + along_y[:, 256:384, :128], along_y[:, 128:256, :128]], axis=1)
    plane, lane = np.arange(PLANES * 128)[:, None] // 128, np.arange(PLANES * 128)[:, None] % 128
    n = np.arange(128)[None, :]
    last = (lane >= 120) & (n == 8 * plane + lane - 120)
    first = (lane < 8) & (n == 8 * plane + lane)
    pack = np.stack([first, last]).astype(np.float32)
    unpack = np.concatenate([last.T, first.T], axis=0).astype(np.float32)
    return [np.asarray(t, np.float32).astype(ml_dtypes.bfloat16) for t in (along_x, along_y, pack, unpack, edge_y)]


def hat(distance):
    return jnp.maximum(0.0, 1.0 - jnp.abs(distance))


def kernel(
    vel_hbm, ids, used, pos_hbm, bx_hbm, by_hbm, pack_hbm, unpack_hbm, be_hbm,
    filt, out_recv,
    vel, pos, bx, by, pack, unpack, be,
    rows_first, rows_last, rows_after, rows_before,
    cols_first, cols_last, cols_after, cols_before, corners,
    early, table, blocks,
    pos_send, pos_recv, out_send,
    in_sems, halo_send, halo_recv, pos_sems, out_sems,
):
    ix, iy = lax.axis_index("gx"), lax.axis_index("gy")
    me = ix * GY + iy

    loads = [
        pltpu.make_async_copy(src, dst, in_sems.at[i])
        for i, (src, dst) in enumerate(
            ((pos_hbm, pos), (vel_hbm, vel), (pack_hbm, pack), (unpack_hbm, unpack), (bx_hbm, bx), (by_hbm, by), (be_hbm, be))
        )
    ]
    for load in loads:
        load.start()

    barrier = pltpu.get_barrier_semaphore()

    def device_of(number):
        return number

    def greet(distance):
        pl.semaphore_signal(
            barrier, 1, device_id=device_of((me + distance) & (DEVICES - 1)), device_id_type=LOGICAL
        )

    for near in range(1, 10):
        greet(near)
        greet(DEVICES - near)

    @pl.loop(1, 7)
    def _(step):
        for near in range(1, 10):
            greet(step * 9 + near)
            greet(DEVICES - step * 9 - near)

    greet(DEVICES // 2)

    loads[0].wait()
    for c in range(3):
        pos_send[:, c, :] = pos[c]
    pos_send[:, 3, :] = pos[0]
    pos_recv[me] = pos_send[me]

    for load in loads[1:3]:
        load.wait()
    for pair in range(PLANES // 2):
        for buf, start, part in ((rows_first, 0, 0), (rows_last, ROWS - 16, 8)):
            low = vel[2 * pair, start : start + 16, :].astype(F32)[part : part + 8]
            high = vel[2 * pair + 1, start : start + 16, :].astype(F32)[part : part + 8]
            buf[pair] = jnp.concatenate([low, high], axis=0).astype(BF16)
    for buf, side, start in ((cols_first, 0, 0), (cols_last, 1, COLS - 128)):
        edge = jnp.concatenate([vel[p, :, start : start + 128] for p in range(PLANES)], axis=1)
        buf[...] = jnp.dot(edge, pack[side], preferred_element_type=F32).astype(BF16)

    pl.semaphore_wait(barrier, DEVICES - 1)

    x_next, x_prev = (ix + 1) & (GX - 1), (ix + GX - 1) & (GX - 1)
    y_next, y_prev = (iy + 1) & (GY - 1), (iy + GY - 1) & (GY - 1)
    top, bottom = pl.ds(0, 16), pl.ds(ROWS - 16, 16)
    halo_copies = [
        pltpu.make_async_remote_copy(
            src, dst, halo_send.at[i], halo_recv.at[i], device_id=target, device_id_type=MESH
        )
        for i, (src, dst, target) in enumerate(
            (
                (rows_first, rows_after, (x_prev, iy)),
                (rows_last, rows_before, (x_next, iy)),
                (cols_first, cols_after, (ix, y_prev)),
                (cols_last, cols_before, (ix, y_next)),
                (cols_last.at[bottom], corners.at[0], (x_next, y_next)),
                (cols_last.at[top], corners.at[1], (x_prev, y_next)),
                (cols_first.at[bottom], corners.at[2], (x_next, y_prev)),
                (cols_first.at[top], corners.at[3], (x_prev, y_prev)),
            )
        )
    ]
    for copy in halo_copies:
        copy.start()

    def send_place(distance):
        other = (me + distance) & (DEVICES - 1)
        pltpu.make_async_remote_copy(
            pos_send.at[other], pos_recv.at[me], pos_sems.at[0], pos_sems.at[1],
            device_id=device_of(other), device_id_type=LOGICAL,
        ).start()

    send_place(DEVICES // 2)

    @pl.loop(0, 7)
    def _(step):
        for near in range(1, 10):
            send_place(step * 9 + near)
            send_place(DEVICES - step * 9 - near)

    for load in loads[3:]:
        load.wait()

    def put(width, pair, results, first_row, first_column):
        for parity, got in enumerate(results):
            filt[
                width * PLANES + 2 * pair + parity,
                first_row : first_row + got.shape[0],
                first_column : first_column + got.shape[1],
            ] = got.astype(BF16)
        for block_row in range(results[0].shape[0] // 8):
            both = jnp.concatenate([got[8 * block_row : 8 * block_row + 8] for got in results], axis=0).astype(BF16)
            for tile in range(results[0].shape[1] // 128):
                table[
                    (first_row // 8 + block_row) * 4 + first_column // 128 + tile, width * (PLANES // 2) + pair
                ] = both[:, 128 * tile : 128 * tile + 128]

    @pl.loop(0, PLANES // 2)
    def _(pair):
        whole = []
        for parity in range(2):
            whole.append(
                jnp.dot(bx[2, :, :ROWS], vel[2 * pair + parity], preferred_element_type=F32).astype(BF16)
            )
            early[2 * pair + parity] = whole[parity]
        for width in range(2):
            results = [
                jnp.dot(w[width * ROWS : (width + 1) * ROWS], by[width], preferred_element_type=F32) for w in whole
            ]
            put(width, pair, results, 0, 128)

    for copy in halo_copies:
        copy.wait_recv()

    packed = jnp.concatenate(
        [
            jnp.concatenate([cols_before[...], corners[0], corners[1]], axis=0),
            jnp.concatenate([cols_after[...], corners[2], corners[3]], axis=0),
        ],
        axis=1,
    )
    lane_of = lax.broadcasted_iota(jnp.int32, (128, 128), 1).astype(BF16)
    aside = jnp.dot(bx[2], packed, preferred_element_type=F32).astype(BF16)

    @pl.loop(0, PLANES // 2)
    def _(pair):
        lanes = pl.ds(pl.multiple_of(256 * pair, 256), 256)
        edges = jnp.dot(aside, unpack[:, lanes], preferred_element_type=F32).astype(BF16)
        smooth, tips = [], []
        for parity in range(2):
            tall = jnp.concatenate([vel[2 * pair + parity], rows_before[pair], rows_after[pair]], axis=0)
            ends = jnp.concatenate(
                [bx[parity, start : start + 16] for start in (0, ROWS - 16, ROWS, 2 * ROWS - 16)], axis=0
            )
            late = jnp.dot(ends, tall, preferred_element_type=F32).astype(BF16)
            tips.append(late)
            smooth.append(
                [
                    jnp.concatenate(
                        [
                            late[32 * width : 32 * width + 16],
                            early[2 * pair + parity, width * ROWS + 16 : width * ROWS + ROWS - 16],
                            late[32 * width + 16 : 32 * width + 32],
                        ],
                        axis=0,
                    )
                    for width in range(2)
                ]
            )
        for width in range(2):
            part = slice(width * ROWS, (width + 1) * ROWS)
            middle = [
                jnp.dot(late[32 * width : 32 * width + 32], by[width], preferred_element_type=F32) for late in tips
            ]
            put(width, pair, [got[:16] for got in middle], 0, 128)
            put(width, pair, [got[16:] for got in middle], ROWS - 16, 128)
            for side in range(2):
                results = []
                for parity in range(2):
                    edge = edges[part, 128 * parity : 128 * parity + 128]
                    inner = smooth[parity][width]
                    if side == 0:
                        beside, own = jnp.where(lane_of < 8.0, inner[:, 128:256], edge), inner[:, :128]
                    else:
                        beside, own = jnp.where(lane_of >= 120.0, inner[:, 256:384], edge), inner[:, 384:]
                    wide = jnp.concatenate([beside, own], axis=1)
                    results.append(jnp.dot(wide, be[width], preferred_element_type=F32))
                put(width, pair, results, 0, 384 * side)

    square = lambda axis: lax.broadcasted_iota(jnp.int32, (128, 128), axis)
    unit = jnp.where(square(0) == square(1), 1.0, 0.0).astype(BF16)

    @pl.loop(0, 64 // TURN)
    def _(step):
        for part in range(TURN):
            tile = step * TURN + part
            if True:
                turned = table[tile].reshape(192, 128).T.astype(F32)
            else:
                turned = lax.dot_general(
                    unit, table[tile].reshape(192, 128), (((1,), (1,)), ((), ())), preferred_element_type=F32
                )
            blocks[pl.ds(tile * 16, 16)] = turned.reshape(16, 8, 192)

    others = pl.ds(0, DEVICES - 1)
    pltpu.make_async_remote_copy(
        pos_send.at[others], pos_recv.at[others], pos_sems.at[0], pos_sems.at[1],
        device_id=(x_next, iy), device_id_type=MESH,
    ).wait()

    lane_slot = lax.shift_right_logical(lax.broadcasted_iota(jnp.int32, (1, 128), 1), 5)
    rows8 = lax.broadcasted_iota(jnp.int32, (8, 128), 0).astype(F32)
    empty = jnp.zeros((32, 128), BF16)

    def sample(owners):
        weights = []
        listed = [blocks[ids[q, owner]] for owner in owners for q in range(CAP)]
        for u, owner in enumerate(owners):
            spot = pos_recv[owner]
            weight_y = jnp.where(lane_slot < used[0, owner], hat(rows8 - 7.0 * spot[1:2]), 0.0)
            mine = jnp.concatenate(
                [jnp.where(lane_slot == q, weight_y, 0.0) for q in range(CAP)], axis=0
            ).astype(BF16)
            weights.append(jnp.concatenate([mine if v == u else empty for v in range(GROUP)], axis=0))
        picked = lax.dot_general(
            jnp.concatenate(listed, axis=0).astype(BF16),
            jnp.concatenate(weights, axis=1),
            (((0,), (0,)), ((), ())),
            preferred_element_type=F32,
        )
        for u, owner in enumerate(owners):
            spot = pos_recv[owner]
            along_x, along_z = 7.0 * spot[0:1], 3.0 * spot[2:3]
            mine = picked[:, 128 * u : 128 * u + 128].reshape(6, 4, 8, 128)
            weight_x = hat(rows8 - along_x)
            total = mine[:, 0] * (weight_x * hat(along_z))
            for z in range(1, 4):
                total = total + mine[:, z] * (weight_x * hat(along_z - float(z)))
            out_send[owner] = jnp.sum(total, axis=1)

    def reply(owner):
        pltpu.make_async_remote_copy(
            out_send.at[owner], out_recv.at[me], out_sems.at[0], out_sems.at[1],
            device_id=device_of(owner), device_id_type=LOGICAL,
        ).start()

    def batch(number):
        steps = [number * BATCH + k for k in range(BATCH)]
        codes = [
            (j & 64) | ((j & 4) << 2) | ((j & 16) >> 3) | ((j & 1) << 5) | (j & 8) | ((j & 32) >> 5) | ((j & 2) << 1)
            for j in steps
        ]
        return [me ^ (((j ^ 86) & 86) | ((j ^ (j >> 1)) & 41)) for j in codes]

    def sample_batch(owners):
        for start in range(0, BATCH, GROUP):
            sample(owners[start : start + GROUP])

    batches = DEVICES // BATCH

    @pl.loop(0, batches - 1)
    def _(number):
        owners = batch(number)
        sample_batch(owners)
        for owner in owners:
            reply(owner)

    owners = batch(batches - 1)
    sample_batch(owners)
    for owner in owners[:-1]:
        reply(owner)
    out_recv[me] = out_send[me]

    for copy in halo_copies:
        copy.wait_send()
    pltpu.make_async_remote_copy(
        out_send.at[others], out_recv.at[others], out_sems.at[0], out_sems.at[1],
        device_id=(x_next, iy), device_id_type=MESH,
    ).wait()


def finish(filt, got, filt_out, samp_out, landed, samp, sems):
    first = pltpu.make_async_copy(got, landed, sems.at[0])
    second = pltpu.make_async_copy(filt, filt_out, sems.at[1])
    first.start()
    second.start()
    first.wait()
    for c in range(6):
        samp[c] = landed[:, c, :]
    third = pltpu.make_async_copy(samp, samp_out, sems.at[2])
    third.start()
    third.wait()
    second.wait()


def body(velocity, block_ids, counts, positions):
    tables = [jnp.asarray(t) for t in constant_tables()]
    hbm = pl.BlockSpec(memory_space=pl.ANY)
    fixed = pl.BlockSpec(memory_space=pltpu.HBM)
    smem = pl.BlockSpec(memory_space=pltpu.SMEM)
    vmem = pl.BlockSpec(memory_space=pltpu.VMEM)
    filtered, landed = pl.pallas_call(
        kernel,
        out_shape=(
            pltpu.VMEM((2 * PLANES, ROWS, COLS), BF16),
            pltpu.VMEM((DEVICES, 6, 128), F32),
        ),
        in_specs=[fixed, smem, smem, fixed, fixed, fixed, fixed, fixed, fixed],
        out_specs=(vmem, vmem),
        scratch_shapes=[
            pltpu.VMEM((PLANES, ROWS, COLS), BF16),
            pltpu.VMEM((3, DEVICES, 128), F32),
            *[pltpu.VMEM(t.shape, BF16) for t in tables],
            *[pltpu.VMEM((PLANES // 2, 16, COLS), BF16)] * 4,
            *[pltpu.VMEM((ROWS, 128), BF16)] * 4,
            pltpu.VMEM((4, 16, 128), BF16),
            pltpu.VMEM((PLANES, 2 * ROWS, COLS), BF16),
            pltpu.VMEM((64, 12, 16, 128), BF16),
            pltpu.VMEM((1024, 8, 192), F32),
            pltpu.VMEM((DEVICES, 4, 128), F32),
            pltpu.VMEM((DEVICES, 4, 128), F32),
            pltpu.VMEM((DEVICES, 6, 128), F32),
            pltpu.SemaphoreType.DMA((7,)),
            pltpu.SemaphoreType.DMA((8,)),
            pltpu.SemaphoreType.DMA((8,)),
            pltpu.SemaphoreType.DMA((2,)),
            pltpu.SemaphoreType.DMA((2,)),
        ],
        compiler_params=pltpu.CompilerParams(
            collective_id=0, has_side_effects=True, vmem_limit_bytes=60 * 1024 * 1024
        ),
        name="filter_and_sample",
    )(
        velocity.reshape(PLANES, ROWS, COLS),
        block_ids.reshape(DEVICES, CAP).T,
        counts.reshape(1, DEVICES),
        positions.reshape(3, DEVICES, 128),
        *tables,
    )
    filtered, sampled = pl.pallas_call(
        finish,
        out_shape=(
            jax.ShapeDtypeStruct((2 * PLANES, ROWS, COLS), BF16),
            jax.ShapeDtypeStruct((6, DEVICES, 128), F32),
        ),
        in_specs=[hbm, hbm],
        out_specs=(hbm, hbm),
        scratch_shapes=[
            pltpu.VMEM((DEVICES, 6, 128), F32),
            pltpu.VMEM((6, DEVICES, 128), F32),
            pltpu.SemaphoreType.DMA((3,)),
        ],
        compiler_params=pltpu.CompilerParams(vmem_limit_bytes=2 * 1024 * 1024),
        name="finish",
    )(filtered, landed)
    return filtered.reshape(2, 3, 4, ROWS, COLS), sampled.reshape(2, 3, 1, 1, DEVICES, 128)


def solution(mesh):
    return jax.shard_map(
        body,
        mesh=mesh,
        in_specs=(
            P(None, None, "gx", "gy"),
            P("gx", "gy", None, None),
            P("gx", "gy", None),
            P(None, "gx", "gy", None, None),
        ),
        out_specs=(P(None, None, None, "gx", "gy"), P(None, None, "gx", "gy", None, None)),
        check_vma=False,
    )
```
